32 devices in a mesh: group: 2 (over core), ctx: 4 (over y, x), tp: 4 (over z).
Axes of the slice: x: 2, y: 2, z: 4, core: 2. Of those that a mesh axis runs over, the one named last changes fastest.
Arguments:
- activations: bfloat16 [1024, 8192], P(('group', 'ctx')), may hold values from -6 to 6
- queries: bfloat16 [1024, 4096], P(('group', 'ctx'), 'tp'), may hold values from -400 to 400
- out_grad: bfloat16 [1024, 4096], P(('group', 'ctx'), 'tp'), may hold values from -6 to 6
- key_weight: bfloat16 [8192, 512], P('ctx', 'tp'), may hold values from -0.0625 to 0.0625
- value_weight: bfloat16 [8192, 512], P('ctx', 'tp'), may hold values from -0.0625 to 0.0625
- sessions: int32 [4, 128], P('ctx'), may hold values from 0 to 3, never falling along the last dimension, each value on 1 to 64 neighbouring positions
Outputs:
- attention: bfloat16 [1024, 4096], P(('group', 'ctx'), 'tp')
- query_grad: bfloat16 [1024, 4096], P(('group', 'ctx'), 'tp')
- key_weight_grad: float32 [8192, 512], P(('group', 'ctx'), 'tp')
- value_weight_grad: float32 [8192, 512], P(('group', 'ctx'), 'tp')
- input_grad: bfloat16 [1024, 8192], P(('group', 'ctx'), 'tp')
The draws below stay inside these ranges and needn't reach their ends.
Inputs may be any that keep to these rules, and one draw needn't show every extreme that they name: `sessions`: each row never falls; every session in a row has 1 to 64 tokens, and one session of each row has exactly that many.
All inputs are finite; a program needn't handle non-finite values.
Results may differ from the reference program's by a relative error of at most 0.025.
The reference program's roundings to bfloat16 on the way count: a program that leaves them out, or rounds other values in their place, can miss the bound.
Values may be sent and summed in bfloat16 or wider, within the bound.
A program may use at most 64 MiB of HBM per device.

```python
import math
import jax
import jax.numpy as jnp
import numpy as np
from jax import lax

D = 8192
HQ = 32
KVH = 4
HD = 128
SESS = 4
TOK_DEV = 128
TOKENS = 1024
N_CTX = 4


def draw_queries(key, part):
    drawn_values = jax.random.normal(jax.random.fold_in(key, 11), (TOKENS, HQ * HD), jnp.float32)
    drawn_values = jnp.clip(drawn_values, -6.0, 6.0)
    return drawn_values.astype(jnp.bfloat16)


def steps_of(stream_key, dims, shards, low, largest):
    def one(dim, shards_of):
        heights = jax.random.uniform(jax.random.fold_in(jax.random.fold_in(stream_key, 6), dim), (shards_of,), jnp.float32, low / len(shards), largest / len(shards))
        return jnp.repeat(jnp.exp(heights), dims[dim] // shards_of).reshape((-1,) + (1,) * (len(dims) - dim - 1))

    loudness = one(*shards[0])
    for cut in shards[1:]:
        loudness = loudness * one(*cut)
    return loudness


def split_up(amount, total, limit, lean):
    portions = [(1 << 20) // math.isqrt(grade ** lean) + 1 for grade in range(2, amount + 1)]
    spare, counts = total - limit - (amount - 1), [1] * (amount - 1)
    while spare > 0:
        free = [i for i in range(amount - 1) if counts[i] < limit]
        pool, budget = sum([portions[i] for i in free]), spare
        for i in free:
            addition = min(limit - counts[i], max(1, budget * portions[i] // pool), spare)
            counts[i] = counts[i] + addition
            spare = spare - addition
    return np.array([limit] + counts)


def uneven_parts(stream_key, count, total, limit, skew):
    if count == 2:
        one = jax.random.randint(stream_key, (), max(1, total - limit), min(limit, total - 1) + 1)
        return jnp.stack([one, total - one])
    tallies = jnp.asarray(split_up(count, total, limit, skew), jnp.int32)
    pairs = (count - 1) // 2
    source_of, sink = tallies[1:1 + 2 * pairs:2], tallies[2:2 + 2 * pairs:2]
    room = jnp.minimum(source_of - 1, limit - sink)
    shifted = jax.random.randint(jax.random.fold_in(stream_key, 1), (pairs,), 0, 1 << 20) % (room + 1)
    tallies = tallies.at[1:1 + 2 * pairs:2].set(source_of - shifted).at[2:2 + 2 * pairs:2].set(sink + shifted)
    return tallies[jax.random.permutation(jax.random.fold_in(stream_key, 2), count)]


def scatter_about(key, dims, width, bound, split=(), held_as=jnp.bfloat16):
    result = jax.random.normal(key, dims, jnp.float32) * width
    if len(split) > 0:
        result = steps_of(key, dims, split, -0.22, 0.18) * result
    return jnp.clip(result, min=-bound, max=bound).astype(held_as)


def setup_inputs(seed: int = 0) -> dict:
    arg_keys = jax.random.split(jax.random.key(seed), 7)
    activations = scatter_about(arg_keys[0], (TOKENS, D), 1.0, 6.0, ((0, 8),))
    queries = draw_queries(jax.random.fold_in(arg_keys[6], 71), 0)
    out_grad = scatter_about(arg_keys[2], (TOKENS, HQ * HD), 1.0, 6.0, ((0, 8), (1, 4)))
    key_weight = scatter_about(arg_keys[3], (D, KVH * HD), D ** -0.5, 0.0625, ((0, 4), (1, 4)))
    value_weight = scatter_about(arg_keys[4], (D, KVH * HD), D ** -0.5, 0.0625, ((0, 4), (1, 4)))
    sessions = jax.vmap(lambda own: jnp.searchsorted(jnp.cumsum(uneven_parts(own, SESS, TOK_DEV, TOK_DEV // 2, 0)), jnp.arange(TOK_DEV), side="right"))(jax.random.split(arg_keys[5], N_CTX)).reshape((N_CTX, TOK_DEV)).astype(jnp.int32)
    return dict(activations=activations, queries=queries, out_grad=out_grad, key_weight=key_weight, value_weight=value_weight, sessions=sessions)


THETA = 500000.0

def rotate(vector, positions, turn_sign):
    half_dim = HD // 2
    frequency = THETA ** (-2.0 * jnp.arange(half_dim, dtype=jnp.float32) / HD)
    angles = positions.astype(jnp.float32)[:, None] * frequency[None, :]
    cosine = jnp.cos(angles)[:, None, :]
    sine_table = turn_sign * jnp.sin(angles)[:, None, :]
    shaped = vector.reshape(vector.shape[0], -1, HD)
    first_half = shaped[..., :half_dim]
    second_half = shaped[..., half_dim:]
    turned = jnp.concatenate([first_half * cosine - second_half * sine_table, second_half * cosine + first_half * sine_table], -1)
    return turned.reshape(vector.shape)

def head_pass(rotated_queries, key_rows, value_rows, out_grad, allowed, head_index):
    score_scale = 1.0 / math.sqrt(HD)
    kv_head = head_index // (HQ // KVH)
    query_head = lax.dynamic_slice_in_dim(rotated_queries, head_index * HD, HD, 1)
    key_head = lax.dynamic_slice_in_dim(key_rows, kv_head * HD, HD, 1)
    value_head = lax.dynamic_slice_in_dim(value_rows, kv_head * HD, HD, 1)
    grad_head = lax.dynamic_slice_in_dim(out_grad, head_index * HD, HD, 1)
    scores = jnp.dot(query_head, key_head.T, preferred_element_type=jnp.float32) * score_scale
    scores = jnp.where(allowed, scores, -jnp.inf)
    log_total = jax.nn.logsumexp(scores, axis=1)
    weights = jnp.exp(scores - log_total[:, None])
    rounded = weights.astype(jnp.bfloat16)
    attended = jnp.dot(rounded, value_head, preferred_element_type=jnp.float32).astype(jnp.bfloat16)
    out_dot = lax.optimization_barrier(jnp.sum(grad_head.astype(jnp.float32) * attended.astype(jnp.float32), 1))
    prob_grad = jnp.dot(grad_head, value_head.T, preferred_element_type=jnp.float32)
    score_grad = (weights * (prob_grad - out_dot[:, None])).astype(jnp.bfloat16)
    query_grad = jnp.dot(score_grad, key_head, preferred_element_type=jnp.float32) * score_scale
    key_grad = jnp.dot(score_grad.T, query_head, preferred_element_type=jnp.float32) * score_scale
    value_grad = jnp.dot(rounded.T, grad_head, preferred_element_type=jnp.float32)
    return (attended, query_grad, key_grad, value_grad)

def attend(rotated_queries, key_rows, value_rows, out_grad, allowed):
    row_count = rotated_queries.shape[0]
    head_list = jnp.arange(HQ, dtype=jnp.int32)
    attended, query_grad, key_grad, value_grad = lax.map(lambda head_index: head_pass(rotated_queries, key_rows, value_rows, out_grad, allowed, head_index), head_list)
    attended = attended.transpose(1, 0, 2).reshape(row_count, HQ * HD)
    query_grad = query_grad.transpose(1, 0, 2).reshape(row_count, HQ * HD)
    key_grad = key_grad.reshape(KVH, HQ // KVH, row_count, HD).sum(1).transpose(1, 0, 2).reshape(row_count, KVH * HD)
    value_grad = value_grad.reshape(KVH, HQ // KVH, row_count, HD).sum(1).transpose(1, 0, 2).reshape(row_count, KVH * HD)
    return (attended, query_grad, key_grad, value_grad)

def short_blocks(array, long_rows):
    return array[long_rows:].reshape(N_CTX, TOK_DEV, array.shape[1])

def reference(activations, queries, out_grad, key_weight, value_weight, sessions):
    long_rows = N_CTX * TOK_DEV
    all_rows = jnp.arange(TOKENS, dtype=jnp.int32)
    positions = jnp.where(all_rows < long_rows, all_rows, all_rows % TOK_DEV)
    key_rows = rotate(jnp.dot(activations, key_weight, preferred_element_type=jnp.float32), positions, 1.0).astype(jnp.bfloat16)
    value_rows = jnp.dot(activations, value_weight, preferred_element_type=jnp.float32).astype(jnp.bfloat16)
    rotated = rotate(queries.astype(jnp.float32), positions, 1.0).astype(jnp.bfloat16)
    causal = all_rows[:long_rows, None] >= all_rows[None, :long_rows]
    long_part = attend(rotated[:long_rows], key_rows[:long_rows], value_rows[:long_rows], out_grad[:long_rows], causal)
    local_rows = jnp.arange(TOK_DEV, dtype=jnp.int32)
    short_allowed = (local_rows[None, :, None] >= local_rows[None, None, :]) & (sessions[:, :, None] == sessions[:, None, :])
    short_part = jax.vmap(attend)(short_blocks(rotated, long_rows), short_blocks(key_rows, long_rows), short_blocks(value_rows, long_rows), short_blocks(out_grad, long_rows), short_allowed)
    merged = [jnp.concatenate([long_piece, short_piece.reshape(-1, short_piece.shape[-1])], 0) for long_piece, short_piece in zip(long_part, short_part)]
    attention, query_raw, key_raw, value_raw = merged
    query_grad = rotate(query_raw, positions, -1.0).astype(jnp.bfloat16)
    key_grad = rotate(key_raw, positions, -1.0).astype(jnp.bfloat16)
    value_grad = value_raw.astype(jnp.bfloat16)
    key_weight_grad = jnp.dot(activations.T, key_grad, preferred_element_type=jnp.float32)
    value_weight_grad = jnp.dot(activations.T, value_grad, preferred_element_type=jnp.float32)
    input_grad = (jnp.dot(key_grad, key_weight.T, preferred_element_type=jnp.float32) + jnp.dot(value_grad, value_weight.T, preferred_element_type=jnp.float32)).astype(jnp.bfloat16)
    return (attention, query_grad, key_weight_grad, value_weight_grad, input_grad)
```

```python
import functools
import math

import jax
import jax.numpy as jnp
from jax import lax
from jax.experimental import pallas as pl
from jax.experimental.pallas import tpu as pltpu
from jax.sharding import PartitionSpec as P

HD = 128
THETA = 500000.0
BF = jnp.bfloat16
F32 = jnp.float32
MESH = pl.DeviceIdType.MESH


def dot(a, b, dims):
    return lax.dot_general(a, b, (dims, ((), ())), preferred_element_type=F32)


def kernel(
    G, C, T,
    act_hbm, q_hbm, do_hbm, wk_hbm, wv_hbm, ses_hbm,
    att_ref, dq_ref, kwg_ref, vwg_ref, ig_ref,
    wall, w2, act, q_in, do_in, ses, arecv, qs, dos, kv, scores, dkv, grecv,
    kvg, kvg_tp, cos_ref, sin_ref, proj, dq_acc,
    loc, w_s, w_r, sb_s, sb_r, z_s, z_r, zf_s, zf_r, a_s, a_r, k_s, k_r,
    d_s, d_r, p_s, p_r, t_s, t_r,
):
    g = lax.axis_index("group")
    c = lax.axis_index("ctx")
    t = lax.axis_index("tp")
    R = act_hbm.shape[0]
    D = act_hbm.shape[1]
    WR = wk_hbm.shape[0]
    CR = min(WR, 512)
    NCH = WR // CR
    DB = D // (G * C)
    DT = D // T
    NK = DT // CR
    H = q_hbm.shape[1] // HD
    scale = 1.0 / math.sqrt(HD)
    is_long = g == 0
    lanes = pl.ds(pl.multiple_of(g * HD, HD), HD)
    olanes = pl.ds(pl.multiple_of((1 - g) * HD, HD), HD)

    def remote(src, dst, ss, rs, **dev):
        return pltpu.make_async_remote_copy(
            src_ref=src, dst_ref=dst, send_sem=ss, recv_sem=rs, device_id=dev, device_id_type=MESH
        )

    def loop(n, f, first=0):
        def step(i, carry):
            f(i)
            return carry

        lax.fori_loop(first, n, step, 0)

    own_rows = pl.ds(pl.multiple_of(c * WR, WR), WR)
    locals_ = [
        pltpu.make_async_copy(wk_hbm, wall.at[own_rows, pl.ds(0, HD)], loc.at[0]),
        pltpu.make_async_copy(wv_hbm, wall.at[own_rows, pl.ds(HD, HD)], loc.at[1]),
        pltpu.make_async_copy(act_hbm, act, loc.at[2]),
        pltpu.make_async_copy(q_hbm, q_in, loc.at[3]),
        pltpu.make_async_copy(do_hbm, do_in, loc.at[4]),
        pltpu.make_async_copy(ses_hbm, ses, loc.at[5]),
    ]
    for one in locals_:
        one.start()

    barrier = pltpu.get_barrier_semaphore()
    me = g * C + c

    def greet_plane(i):
        b = lax.rem(me + i, G * C)
        pl.semaphore_signal(
            barrier, inc=1, device_id={"group": b // C, "ctx": lax.rem(b, C)}, device_id_type=MESH
        )

    def greet_tp(i):
        pl.semaphore_signal(
            barrier, inc=1, device_id={"tp": lax.rem(t + i, T)}, device_id_type=MESH
        )

    loop(G * C, greet_plane, 1)
    loop(T, greet_tp, 1)
    pl.semaphore_wait(barrier, G * C - 1 + T - 1)
    locals_[0].wait()
    locals_[1].wait()

    def rows_of(owner, ch):
        return pl.ds(pl.multiple_of(owner * WR + ch * CR, CR), CR)

    def w_copy(owner, ch, d):
        place = wall.at[rows_of(owner, ch), lanes]
        return remote(
            place, place, w_s.at[d, ch], w_r.at[owner, ch], ctx=lax.rem(c + d, C)
        )

    def send_w(i):
        w_copy(c, i // (C - 1), lax.rem(i, C - 1) + 1).start()

    loop(NCH * (C - 1), send_w)

    def sib_copy(owner, ch, which):
        place = wall.at[rows_of(owner, ch), which]
        return remote(place, place, sb_s.at[owner, ch], sb_r.at[owner, ch], group=1 - g)

    def z_target(owner, ch):
        first = owner * WR + ch * CR
        return first // DT, lax.rem(first, DT) // CR

    def z_start(owner, ch):
        to, piece = z_target(owner, ch)

        @pl.when(to != t)
        def _():
            z_copy(owner, ch, to, t, piece).start()

    def z_copy(owner, ch, to, head, piece):
        return remote(
            wall.at[rows_of(owner, ch), lanes],
            w2.at[head, pl.ds(pl.multiple_of(piece * CR, CR), CR), lanes],
            z_s.at[owner, ch], z_r.at[head, piece], tp=to,
        )

    def own_z(ch):
        z_start(c, ch)

    loop(NCH, own_z)

    lane = lax.broadcasted_iota(jnp.int32, (R, HD), 1)
    row = lax.broadcasted_iota(jnp.int32, (R, HD), 0)
    half = lax.rem(lane, HD // 2).astype(F32)
    freq = jnp.exp(half * (-2.0 * math.log(THETA) / HD))
    angle = (row + jnp.where(is_long, c * R, 0)).astype(F32) * freq
    cos_ref[...] = jnp.cos(angle)
    sin_ref[...] = jnp.where(lane < HD // 2, -1.0, 1.0) * jnp.sin(angle)

    def rope(u, sign):
        return u * cos_ref[...] + pltpu.roll(u, HD // 2, 1) * (sin_ref[...] * sign)

    for one in locals_[2:]:
        one.wait()
    for h in range(H):
        cols = slice(h * HD, (h + 1) * HD)
        qs[h] = rope(q_in[:, cols].astype(F32), 1.0).astype(BF)
        dos[h] = do_in[:, cols]

    proj[...] = jnp.zeros_like(proj)

    def project(owner, ch):
        first = pl.multiple_of(owner * WR + ch * CR, CR)
        proj[...] += dot(act[:, pl.ds(first, CR)], wall[rows_of(owner, ch), :], ((1,), (0,)))

    def own_project(ch):
        project(c, ch)

    loop(NCH, own_project)

    def arrived(i):
        ch = i // (C - 1)
        owner = lax.rem(c + C - (lax.rem(i, C - 1) + 1), C)
        w_copy(owner, ch, 1).wait_recv()
        sib_copy(owner, ch, lanes).start()
        z_start(owner, ch)

    def use(i):
        ch = i // (C - 1)
        owner = lax.rem(c + C - (lax.rem(i, C - 1) + 1), C)
        sib_copy(owner, ch, olanes).wait_recv()
        project(owner, ch)

    def chunk(ch):
        loop((ch + 1) * (C - 1), arrived, ch * (C - 1))

        @pl.when(ch > 0)
        def _():
            loop(ch * (C - 1), use, (ch - 1) * (C - 1))

    loop(NCH, chunk)

    def a_copy(i, slot):
        b = lax.rem(me + i, G * C)
        return remote(
            act.at[:, pl.ds(pl.multiple_of(b * DB, DB), DB)],
            arecv.at[pl.ds(pl.multiple_of(slot * R, R), R), :],
            a_s.at[i], a_r.at[slot],
            group=b // C, ctx=lax.rem(b, C),
        )

    def a_start(i):
        a_copy(i, me).start()

    loop(G * C, a_start, 1)
    own_a = pltpu.make_async_copy(
        act.at[:, pl.ds(pl.multiple_of(me * DB, DB), DB)],
        arecv.at[pl.ds(pl.multiple_of(me * R, R), R), :],
        loc.at[0],
    )
    own_a.start()
    loop(NCH * (C - 1), use, (NCH - 1) * (C - 1))

    kv[c, :, :HD] = rope(proj[:, :HD], 1.0).astype(BF)
    kv[c, :, HD:] = proj[:, HD:].astype(BF)

    def kv_copy(owner, to):
        return remote(kv.at[owner], kv.at[owner], k_s.at[to], k_r.at[owner], ctx=to)

    @pl.when(is_long)
    def _():
        loop(C, lambda to: kv_copy(c, to).start(), c + 1)

    first_block = jnp.where(is_long, 0, c)
    srow = jnp.broadcast_to(ses[...].astype(F32), (R, R))
    same = (srow == srow.T) | is_long
    q_pos = lax.broadcasted_iota(jnp.int32, (R, R), 0)
    k_pos = lax.broadcasted_iota(jnp.int32, (R, R), 1)
    queries = qs[...].reshape(H * R, HD)

    def score_pass(i, top):
        j = c - i + first_block * 0

        @pl.when(j != c)
        def _():
            kv_copy(j, 0).wait_recv()

        s = dot(queries, kv[j, :, :HD], ((1,), (1,))) * scale
        allowed = same & (k_pos <= q_pos + (c - j) * R)
        s = jnp.where(allowed[None], s.reshape(H, R, R), -jnp.inf).reshape(H * R, R)
        scores[j] = s
        return jnp.maximum(top, jnp.max(s, 1, keepdims=True))

    count = c + 1 - first_block
    top = lax.fori_loop(0, count, score_pass, jnp.full((H * R, 1), -jnp.inf, F32))

    def sum_pass(j, total):
        return total + jnp.sum(jnp.exp(scores[j] - top), 1, keepdims=True)

    total = lax.fori_loop(first_block, c + 1, sum_pass, jnp.zeros((H * R, 1), F32))
    log_total = top + jnp.log(total)

    dq_acc[...] = jnp.zeros_like(dq_acc)

    def out_pass(j):
        w = jnp.exp(scores[j] - log_total)
        scores[j] = w
        dq_acc[...] += dot(w.astype(BF), kv[j, :, HD:], ((1,), (0,)))

    loop(c + 1, out_pass, first_block)
    attended = dq_acc[...].astype(BF)
    for h in range(H):
        att_ref[:, h * HD:(h + 1) * HD] = attended[h * R:(h + 1) * R]
    grads = dos[...].reshape(H * R, HD)
    out_dot = jnp.sum(grads.astype(F32) * attended.astype(F32), 1, keepdims=True)
    dq_acc[...] = jnp.zeros_like(dq_acc)

    def d_copy(owner, source):
        return remote(dkv.at[owner], grecv.at[source], d_s.at[owner], d_r.at[source], ctx=owner)

    def grad_pass(j):
        w = scores[j]
        prob_grad = dot(grads, kv[j, :, HD:], ((1,), (1,)))
        ds = (w * (prob_grad - out_dot)).astype(BF)
        dkv[j, :, :HD] = dot(ds, queries, ((0,), (0,))) * scale
        dkv[j, :, HD:] = dot(w.astype(BF), grads, ((0,), (0,)))

        @pl.when(j != c)
        def _():
            d_copy(j, c).start()

        dq_acc[...] += dot(ds, kv[j, :, :HD], ((1,), (0,)))

    loop(c + 1, grad_pass, first_block)
    for h in range(H):
        turned = rope(dq_acc[h * R:(h + 1) * R] * scale, -1.0)
        dq_ref[:, h * HD:(h + 1) * HD] = turned.astype(BF)

    proj[...] = dkv[c]

    def add_grad(source):
        d_copy(0, source).wait_recv()
        proj[...] += grecv[source]

    @pl.when(is_long)
    def _():
        loop(C, add_grad, c + 1)

    my_rows = pl.ds(pl.multiple_of(me * R, R), R)
    kvg[my_rows, :HD] = rope(proj[:, :HD], -1.0).astype(BF)
    kvg[my_rows, HD:] = proj[:, HD:].astype(BF)

    def p_copy(i, slot):
        b = lax.rem(me + i, G * C)
        rows = pl.ds(pl.multiple_of(slot * R, R), R)
        return remote(
            kvg.at[rows], kvg.at[rows], p_s.at[i], p_r.at[slot], group=b // C, ctx=lax.rem(b, C)
        )

    def t_copy(i, slot):
        return remote(kvg.at[my_rows], kvg_tp.at[slot], t_s.at[i], t_r.at[slot], tp=lax.rem(t + i, T))

    loop(T, lambda i: t_copy(i, t).start(), 1)
    loop(G * C, lambda i: p_copy(i, me).start(), 1)

    def zf_copy(head, piece, which):
        place = w2.at[head, pl.ds(pl.multiple_of(piece * CR, CR), CR), which]
        return remote(place, place, zf_s.at[head, piece], zf_r.at[head, piece], group=1 - g)

    def z_arrived(i):
        head = lax.rem(t + 1 + i // NK, T)
        piece = lax.rem(i, NK)
        z_copy(0, 0, 0, head, piece).wait_recv()
        zf_copy(head, piece, lanes).start()

    loop((T - 1) * NK, z_arrived)

    own_a.wait()

    def a_wait(i):
        slot = lax.rem(me + i, G * C)
        a_copy(0, slot).wait_recv()
        p_copy(0, slot).wait_recv()

    loop(G * C, a_wait, 1)
    step = min(DB, 256)

    def wgrad(i):
        at = pl.ds(pl.multiple_of(i * step, step), step)
        both = dot(arecv[:, at], kvg[...], ((0,), (0,)))
        kwg_ref[at, :] = both[:, :HD]
        vwg_ref[at, :] = both[:, HD:]

    loop(DB // step, wgrad)

    loop(T, lambda i: t_copy(0, lax.rem(t + i, T)).wait_recv(), 1)

    def z_wait(i):
        zf_copy(lax.rem(t + 1 + i // NK, T), lax.rem(i, NK), olanes).wait_recv()

    loop((T - 1) * NK, z_wait)

    def igrad(i):
        at = pl.multiple_of(i * CR, CR)
        own = wall[pl.ds(pl.multiple_of(t * DT + i * CR, CR), CR), :]
        result = dot(kvg[my_rows, :], own, ((1,), (1,)))
        for d in range(1, T):
            head = lax.rem(t + d, T)
            result += dot(kvg_tp[head], w2[head, pl.ds(at, CR), :], ((1,), (1,)))
        ig_ref[:, pl.ds(at, CR)] = result.astype(BF)

    loop(NK, igrad)

    loop(NCH * (C - 1), lambda i: w_copy(c, i // (C - 1), lax.rem(i, C - 1) + 1).wait_send())

    def sent_chunk(i):
        owner = i // NCH
        ch = lax.rem(i, NCH)

        @pl.when(owner != c)
        def _():
            sib_copy(owner, ch, lanes).wait_send()

        to, piece = z_target(owner, ch)

        @pl.when(to != t)
        def _():
            z_copy(owner, ch, to, t, piece).wait_send()

    loop(C * NCH, sent_chunk)
    loop(G * C, lambda i: a_copy(i, me).wait_send(), 1)
    loop(G * C, lambda i: p_copy(i, me).wait_send(), 1)
    loop(T, lambda i: t_copy(i, t).wait_send(), 1)
    loop((T - 1) * NK, lambda i: zf_copy(
        lax.rem(t + 1 + i // NK, T), lax.rem(i, NK), lanes).wait_send())

    @pl.when(is_long)
    def _():
        loop(C, lambda to: kv_copy(c, to).wait_send(), c + 1)
        loop(c, lambda owner: d_copy(owner, c).wait_send())


def body(sizes, activations, queries, out_grad, key_weight, value_weight, sessions):
    G, C, T = sizes
    R, D = activations.shape
    WR = key_weight.shape[0]
    QC = queries.shape[1]
    H = QC // HD
    CR = min(WR, 512)
    NCH = WR // CR
    DB = D // (G * C)
    DT = D // T
    NK = DT // CR
    any_ = pl.BlockSpec(memory_space=pl.ANY)
    vmem = pl.BlockSpec(memory_space=pltpu.VMEM)
    dma = pltpu.SemaphoreType.DMA
    V = pltpu.VMEM
    return pl.pallas_call(
        functools.partial(kernel, G, C, T),
        out_shape=(
            jax.ShapeDtypeStruct((R, QC), BF),
            jax.ShapeDtypeStruct((R, QC), BF),
            jax.ShapeDtypeStruct((DB, HD), F32),
            jax.ShapeDtypeStruct((DB, HD), F32),
            jax.ShapeDtypeStruct((R, DT), BF),
        ),
        in_specs=[any_] * 6,
        out_specs=(vmem,) * 5,
        scratch_shapes=[
            V((D, 2 * HD), BF), V((T, DT, 2 * HD), BF), V((R, D), BF), V((R, QC), BF),
            V((R, QC), BF), V((1, R), jnp.int32), V((G * C * R, DB), BF), V((H, R, HD), BF),
            V((H, R, HD), BF), V((C, R, 2 * HD), BF), V((C, H * R, R), F32),
            V((C, R, 2 * HD), F32), V((C, R, 2 * HD), F32),
            V((G * C * R, 2 * HD), BF), V((T, R, 2 * HD), BF),
            V((R, HD), F32), V((R, HD), F32), V((R, 2 * HD), F32), V((H * R, HD), F32),
            dma((6,)),
            dma((C, NCH)), dma((C, NCH)), dma((C, NCH)), dma((C, NCH)),
            dma((C, NCH)), dma((T, NK)), dma((T, NK)), dma((T, NK)),
            dma((G * C,)), dma((G * C,)), dma((C,)), dma((C,)),
            dma((C,)), dma((C,)), dma((G * C,)), dma((G * C,)), dma((T,)), dma((T,)),
        ],
        compiler_params=pltpu.CompilerParams(
            collective_id=0, has_side_effects=True, vmem_limit_bytes=58 * 1024 * 1024
        ),
    )(activations, queries, out_grad, key_weight, value_weight, sessions)


def solution(mesh):
    rows = ("group", "ctx")
    sizes = tuple(mesh.shape[name] for name in ("group", "ctx", "tp"))
    return jax.shard_map(
        functools.partial(body, sizes),
        mesh=mesh,
        in_specs=(
            P(rows, None), P(rows, "tp"), P(rows, "tp"),
            P("ctx", "tp"), P("ctx", "tp"), P("ctx", None),
        ),
        out_specs=(P(rows, "tp"),) * 5,
        check_vma=False,
    )
```

```python
import functools
import math

import jax
import jax.numpy as jnp
from jax import lax
from jax.experimental import pallas as pl
from jax.experimental.pallas import tpu as pltpu
from jax.sharding import PartitionSpec as P

HD = 128
THETA = 500000.0
BF = jnp.bfloat16
F32 = jnp.float32
MESH = pl.DeviceIdType.MESH


def dot(a, b, dims):
    return lax.dot_general(a, b, (dims, ((), ())), preferred_element_type=F32)


def kernel(
    G, C, T,
    act_hbm, q_hbm, do_hbm, wk_hbm, wv_hbm, ses_hbm,
    att_ref, dq_ref, kwg_ref, vwg_ref, ig_ref,
    wall, w2, act, q_in, do_in, ses, arecv, qs, dos, kv, scores, dkv, grecv,
    kvg, kvg_tp, cos_ref, sin_ref, proj, dq_acc,
    loc, w_s, w_r, sb_s, sb_r, z_s, z_r, zf_s, zf_r, a_s, a_r, k_s, k_r,
    d_s, d_r, p_s, p_r, t_s, t_r,
):
    g = lax.axis_index("group")
    c = lax.axis_index("ctx")
    t = lax.axis_index("tp")
    R = act_hbm.shape[0]
    D = act_hbm.shape[1]
    WR = wk_hbm.shape[0]
    CR = min(WR, 512)
    NCH = WR // CR
    DB = D // (G * C)
    DT = D // T
    NK = DT // CR
    H = q_hbm.shape[1] // HD
    scale = 1.0 / math.sqrt(HD)
    is_long = g == 0
    lanes = pl.ds(pl.multiple_of(g * HD, HD), HD)
    olanes = pl.ds(pl.multiple_of((1 - g) * HD, HD), HD)

    def remote(src, dst, ss, rs, **dev):
        return pltpu.make_async_remote_copy(
            src_ref=src, dst_ref=dst, send_sem=ss, recv_sem=rs, device_id=dev, device_id_type=MESH
        )

    def loop(n, f, first=0):
        def step(i, carry):
            f(i)
            return carry

        lax.fori_loop(first, n, step, 0)

    own_rows = pl.ds(pl.multiple_of(c * WR, WR), WR)
    locals_ = [
        pltpu.make_async_copy(wk_hbm, wall.at[own_rows, pl.ds(0, HD)], loc.at[0]),
        pltpu.make_async_copy(wv_hbm, wall.at[own_rows, pl.ds(HD, HD)], loc.at[1]),
        pltpu.make_async_copy(act_hbm, act, loc.at[2]),
        pltpu.make_async_copy(q_hbm, q_in, loc.at[3]),
        pltpu.make_async_copy(do_hbm, do_in, loc.at[4]),
        pltpu.make_async_copy(ses_hbm, ses, loc.at[5]),
    ]
    for one in locals_:
        one.start()

    barrier = pltpu.get_barrier_semaphore()
    me = g * C + c

    def greet_plane(i):
        b = lax.rem(me + i, G * C)
        pl.semaphore_signal(
            barrier, inc=1, device_id={"group": b // C, "ctx": lax.rem(b, C)}, device_id_type=MESH
        )

    def greet_tp(i):
        pl.semaphore_signal(
            barrier, inc=1, device_id={"tp": lax.rem(t + i, T)}, device_id_type=MESH
        )

    loop(G * C, greet_plane, 1)
    loop(T, greet_tp, 1)
    pl.semaphore_wait(barrier, G * C - 1 + T - 1)
    locals_[0].wait()
    locals_[1].wait()

    def rows_of(owner, ch):
        return pl.ds(pl.multiple_of(owner * WR + ch * CR, CR), CR)

    def w_copy(owner, ch, d):
        place = wall.at[rows_of(owner, ch), lanes]
        return remote(
            place, place, w_s.at[d, ch], w_r.at[owner, ch], ctx=lax.rem(c + d, C)
        )

    def send_w(i):
        w_copy(c, i // (C - 1), lax.rem(i, C - 1) + 1).start()

    loop(NCH * (C - 1), send_w)

    def sib_copy(owner, ch, which):
        place = wall.at[rows_of(owner, ch), which]
        return remote(place, place, sb_s.at[owner, ch], sb_r.at[owner, ch], group=1 - g)

    def z_target(owner, ch):
        first = owner * WR + ch * CR
        return first // DT, lax.rem(first, DT) // CR

    def z_start(owner, ch):
        to, piece = z_target(owner, ch)

        @pl.when(to != t)
        def _():
            z_copy(owner, ch, to, t, piece).start()

    def z_copy(owner, ch, to, head, piece):
        return remote(
            wall.at[rows_of(owner, ch), lanes],
            w2.at[head, pl.ds(pl.multiple_of(piece * CR, CR), CR), lanes],
            z_s.at[owner, ch], z_r.at[head, piece], tp=to,
        )

    def own_z(ch):
        z_start(c, ch)

    loop(NCH, own_z)

    lane = lax.broadcasted_iota(jnp.int32, (R, HD), 1)
    row = lax.broadcasted_iota(jnp.int32, (R, HD), 0)
    half = lax.rem(lane, HD // 2).astype(F32)
    freq = jnp.exp(half * (-2.0 * math.log(THETA) / HD))
    angle = (row + jnp.where(is_long, c * R, 0)).astype(F32) * freq
    cos_ref[...] = jnp.cos(angle)
    sin_ref[...] = jnp.where(lane < HD // 2, -1.0, 1.0) * jnp.sin(angle)

    def rope(u, sign):
        return u * cos_ref[...] + pltpu.roll(u, HD // 2, 1) * (sin_ref[...] * sign)

    for one in locals_[2:]:
        one.wait()
    for h in range(H):
        cols = slice(h * HD, (h + 1) * HD)
        qs[h] = rope(q_in[:, cols].astype(F32), 1.0).astype(BF)
        dos[h] = do_in[:, cols]

    proj[...] = jnp.zeros_like(proj)

    def project(owner, ch):
        first = pl.multiple_of(owner * WR + ch * CR, CR)
        proj[...] += dot(act[:, pl.ds(first, CR)], wall[rows_of(owner, ch), :], ((1,), (0,)))

    def own_project(ch):
        project(c, ch)

    loop(NCH, own_project)

    def arrived(i):
        ch = i // (C - 1)
        owner = lax.rem(c + C - (lax.rem(i, C - 1) + 1), C)
        w_copy(owner, ch, 1).wait_recv()
        sib_copy(owner, ch, lanes).start()
        z_start(owner, ch)

    def use(i):
        ch = i // (C - 1)
        owner = lax.rem(c + C - (lax.rem(i, C - 1) + 1), C)
        sib_copy(owner, ch, olanes).wait_recv()
        project(owner, ch)

    def chunk(ch):
        loop((ch + 1) * (C - 1), arrived, ch * (C - 1))

        @pl.when(ch > 0)
        def _():
            loop(ch * (C - 1), use, (ch - 1) * (C - 1))

    loop(NCH, chunk)

    def a_copy(i, slot):
        b = lax.rem(me + i, G * C)
        return remote(
            act.at[:, pl.ds(pl.multiple_of(b * DB, DB), DB)],
            arecv.at[pl.ds(pl.multiple_of(slot * R, R), R), :],
            a_s.at[i], a_r.at[slot],
            group=b // C, ctx=lax.rem(b, C),
        )

    def a_start(i):
        a_copy(i, me).start()

    own_a = pltpu.make_async_copy(
        act.at[:, pl.ds(pl.multiple_of(me * DB, DB), DB)],
        arecv.at[pl.ds(pl.multiple_of(me * R, R), R), :],
        loc.at[0],
    )
    own_a.start()
    loop(NCH * (C - 1), use, (NCH - 1) * (C - 1))

    kv[c, :, :HD] = rope(proj[:, :HD], 1.0).astype(BF)
    kv[c, :, HD:] = proj[:, HD:].astype(BF)

    def kv_copy(owner, to):
        return remote(kv.at[owner], kv.at[owner], k_s.at[to], k_r.at[owner], ctx=to)

    @pl.when(is_long)
    def _():
        loop(C, lambda to: kv_copy(c, to).start(), c + 1)

    first_block = jnp.where(is_long, 0, c)
    srow = jnp.broadcast_to(ses[...].astype(F32), (R, R))
    same = (srow == srow.T) | is_long
    q_pos = lax.broadcasted_iota(jnp.int32, (R, R), 0)
    k_pos = lax.broadcasted_iota(jnp.int32, (R, R), 1)
    queries = qs[...].reshape(H * R, HD)

    def score_pass(i, top):
        j = c - i + first_block * 0

        @pl.when(j != c)
        def _():
            kv_copy(j, 0).wait_recv()

        s = dot(queries, kv[j, :, :HD], ((1,), (1,))) * scale
        allowed = same & (k_pos <= q_pos + (c - j) * R)
        s = jnp.where(allowed[None], s.reshape(H, R, R), -jnp.inf).reshape(H * R, R)
        scores[j] = s
        return jnp.maximum(top, jnp.max(s, 1, keepdims=True))

    count = c + 1 - first_block
    top = lax.fori_loop(0, count, score_pass, jnp.full((H * R, 1), -jnp.inf, F32))
    loop(G * C // 2, a_start, 1)

    def sum_pass(j, total):
        return total + jnp.sum(jnp.exp(scores[j] - top), 1, keepdims=True)

    total = lax.fori_loop(first_block, c + 1, sum_pass, jnp.zeros((H * R, 1), F32))
    log_total = top + jnp.log(total)

    dq_acc[...] = jnp.zeros_like(dq_acc)

    def out_pass(j):
        w = jnp.exp(scores[j] - log_total)
        scores[j] = w
        dq_acc[...] += dot(w.astype(BF), kv[j, :, HD:], ((1,), (0,)))

    loop(c + 1, out_pass, first_block)
    attended = dq_acc[...].astype(BF)
    for h in range(H):
        att_ref[:, h * HD:(h + 1) * HD] = attended[h * R:(h + 1) * R]
    grads = dos[...].reshape(H * R, HD)
    out_dot = jnp.sum(grads.astype(F32) * attended.astype(F32), 1, keepdims=True)
    dq_acc[...] = jnp.zeros_like(dq_acc)

    def d_copy(owner, source):
        return remote(dkv.at[owner], grecv.at[source], d_s.at[owner], d_r.at[source], ctx=owner)

    def grad_pass(j):
        w = scores[j]
        prob_grad = dot(grads, kv[j, :, HD:], ((1,), (1,)))
        ds = (w * (prob_grad - out_dot)).astype(BF)
        dkv[j, :, :HD] = dot(ds, queries, ((0,), (0,))) * scale
        dkv[j, :, HD:] = dot(w.astype(BF), grads, ((0,), (0,)))

        @pl.when(j != c)
        def _():
            d_copy(j, c).start()

        dq_acc[...] += dot(ds, kv[j, :, :HD], ((1,), (0,)))

    loop(c + 1, grad_pass, first_block)
    loop(G * C, a_start, G * C // 2)
    for h in range(H):
        turned = rope(dq_acc[h * R:(h + 1) * R] * scale, -1.0)
        dq_ref[:, h * HD:(h + 1) * HD] = turned.astype(BF)

    proj[...] = dkv[c]

    def add_grad(source):
        d_copy(0, source).wait_recv()
        proj[...] += grecv[source]

    @pl.when(is_long)
    def _():
        loop(C, add_grad, c + 1)

    my_rows = pl.ds(pl.multiple_of(me * R, R), R)
    kvg[my_rows, :HD] = rope(proj[:, :HD], -1.0).astype(BF)
    kvg[my_rows, HD:] = proj[:, HD:].astype(BF)

    def p_copy(i, slot):
        b = lax.rem(me + i, G * C)
        rows = pl.ds(pl.multiple_of(slot * R, R), R)
        return remote(
            kvg.at[rows], kvg.at[rows], p_s.at[i], p_r.at[slot], group=b // C, ctx=lax.rem(b, C)
        )

    def t_copy(i, slot):
        return remote(kvg.at[my_rows], kvg_tp.at[slot], t_s.at[i], t_r.at[slot], tp=lax.rem(t + i, T))

    loop(T, lambda i: t_copy(i, t).start(), 1)
    loop(G * C, lambda i: p_copy(i, me).start(), 1)

    def zf_copy(head, piece, which):
        place = w2.at[head, pl.ds(pl.multiple_of(piece * CR, CR), CR), which]
        return remote(place, place, zf_s.at[head, piece], zf_r.at[head, piece], group=1 - g)

    def z_arrived(i):
        head = lax.rem(t + 1 + i // NK, T)
        piece = lax.rem(i, NK)
        z_copy(0, 0, 0, head, piece).wait_recv()
        zf_copy(head, piece, lanes).start()

    loop((T - 1) * NK, z_arrived)

    loop(T, lambda i: t_copy(0, lax.rem(t + i, T)).wait_recv(), 1)

    def z_wait(i):
        zf_copy(lax.rem(t + 1 + i // NK, T), lax.rem(i, NK), olanes).wait_recv()

    loop((T - 1) * NK, z_wait)

    def igrad(i):
        at = pl.multiple_of(i * CR, CR)
        own = wall[pl.ds(pl.multiple_of(t * DT + i * CR, CR), CR), :]
        result = dot(kvg[my_rows, :], own, ((1,), (1,)))
        for d in range(1, T):
            head = lax.rem(t + d, T)
            result += dot(kvg_tp[head], w2[head, pl.ds(at, CR), :], ((1,), (1,)))
        ig_ref[:, pl.ds(at, CR)] = result.astype(BF)

    loop(NK, igrad)

    own_a.wait()

    def a_wait(i):
        slot = lax.rem(me + i, G * C)
        a_copy(0, slot).wait_recv()
        p_copy(0, slot).wait_recv()

    loop(G * C, a_wait, 1)
    step = min(DB, 256)

    def wgrad(i):
        at = pl.ds(pl.multiple_of(i * step, step), step)
        both = dot(arecv[:, at], kvg[...], ((0,), (0,)))
        kwg_ref[at, :] = both[:, :HD]
        vwg_ref[at, :] = both[:, HD:]

    loop(DB // step, wgrad)

    loop(NCH * (C - 1), lambda i: w_copy(c, i // (C - 1), lax.rem(i, C - 1) + 1).wait_send())

    def sent_chunk(i):
        owner = i // NCH
        ch = lax.rem(i, NCH)

        @pl.when(owner != c)
        def _():
            sib_copy(owner, ch, lanes).wait_send()

        to, piece = z_target(owner, ch)

        @pl.when(to != t)
        def _():
            z_copy(owner, ch, to, t, piece).wait_send()

    loop(C * NCH, sent_chunk)
    loop(G * C, lambda i: a_copy(i, me).wait_send(), 1)
    loop(G * C, lambda i: p_copy(i, me).wait_send(), 1)
    loop(T, lambda i: t_copy(i, t).wait_send(), 1)
    loop((T - 1) * NK, lambda i: zf_copy(
        lax.rem(t + 1 + i // NK, T), lax.rem(i, NK), lanes).wait_send())

    @pl.when(is_long)
    def _():
        loop(C, lambda to: kv_copy(c, to).wait_send(), c + 1)
        loop(c, lambda owner: d_copy(owner, c).wait_send())


def copy_kernel(n, *refs):
    sems = refs[2 * n]
    hold = refs[2 * n + 1:]
    come = [pltpu.make_async_copy(refs[k], hold[k], sems.at[k]) for k in range(n)]
    leave = [pltpu.make_async_copy(hold[k], refs[n + k], sems.at[n + k]) for k in range(n)]
    for one in come:
        one.start()
    for k in range(n):
        come[k].wait()
        leave[k].start()
    for one in leave:
        one.wait()


def hand_out(arrays):
    n = len(arrays)
    any_ = pl.BlockSpec(memory_space=pl.ANY)
    return pl.pallas_call(
        functools.partial(copy_kernel, n),
        out_shape=tuple(jax.ShapeDtypeStruct(a.shape, a.dtype) for a in arrays),
        in_specs=[any_] * n,
        out_specs=(any_,) * n,
        scratch_shapes=[pltpu.SemaphoreType.DMA((2 * n,))] + [pltpu.VMEM(a.shape, a.dtype) for a in arrays],
    )(*arrays)


def body(sizes, activations, queries, out_grad, key_weight, value_weight, sessions):
    G, C, T = sizes
    R, D = activations.shape
    WR = key_weight.shape[0]
    QC = queries.shape[1]
    H = QC // HD
    CR = min(WR, 512)
    NCH = WR // CR
    DB = D // (G * C)
    DT = D // T
    NK = DT // CR
    any_ = pl.BlockSpec(memory_space=pl.ANY)
    vmem = pl.BlockSpec(memory_space=pltpu.VMEM)
    dma = pltpu.SemaphoreType.DMA
    V = pltpu.VMEM
    made = pl.pallas_call(
        functools.partial(kernel, G, C, T),
        out_shape=(
            jax.ShapeDtypeStruct((R, QC), BF),
            jax.ShapeDtypeStruct((R, QC), BF),
            jax.ShapeDtypeStruct((DB, HD), F32),
            jax.ShapeDtypeStruct((DB, HD), F32),
            jax.ShapeDtypeStruct((R, DT), BF),
        ),
        in_specs=[any_] * 6,
        out_specs=(vmem,) * 5,
        scratch_shapes=[
            V((D, 2 * HD), BF), V((T, DT, 2 * HD), BF), V((R, D), BF), V((R, QC), BF),
            V((R, QC), BF), V((1, R), jnp.int32), V((G * C * R, DB), BF), V((H, R, HD), BF),
            V((H, R, HD), BF), V((C, R, 2 * HD), BF), V((C, H * R, R), F32),
            V((C, R, 2 * HD), F32), V((C, R, 2 * HD), F32),
            V((G * C * R, 2 * HD), BF), V((T, R, 2 * HD), BF),
            V((R, HD), F32), V((R, HD), F32), V((R, 2 * HD), F32), V((H * R, HD), F32),
            dma((6,)),
            dma((C, NCH)), dma((C, NCH)), dma((C, NCH)), dma((C, NCH)),
            dma((C, NCH)), dma((T, NK)), dma((T, NK)), dma((T, NK)),
            dma((G * C,)), dma((G * C,)), dma((C,)), dma((C,)),
            dma((C,)), dma((C,)), dma((G * C,)), dma((G * C,)), dma((T,)), dma((T,)),
        ],
        compiler_params=pltpu.CompilerParams(
            collective_id=0, has_side_effects=True, vmem_limit_bytes=58 * 1024 * 1024
        ),
    )(activations, queries, out_grad, key_weight, value_weight, sessions)
    return hand_out(made)


def solution(mesh):
    rows = ("group", "ctx")
    sizes = tuple(mesh.shape[name] for name in ("group", "ctx", "tp"))
    return jax.shard_map(
        functools.partial(body, sizes),
        mesh=mesh,
        in_specs=(
            P(rows, None), P(rows, "tp"), P(rows, "tp"),
            P("ctx", "tp"), P("ctx", "tp"), P("ctx", None),
        ),
        out_specs=(P(rows, "tp"),) * 5,
        check_vma=False,
    )
```

```python
import functools
import math

import jax
import jax.numpy as jnp
from jax import lax
from jax.experimental import pallas as pl
from jax.experimental.pallas import tpu as pltpu
from jax.sharding import PartitionSpec as P

HD = 128
THETA = 500000.0
BF = jnp.bfloat16
F32 = jnp.float32
MESH = pl.DeviceIdType.MESH


def dot(a, b, dims):
    return lax.dot_general(a, b, (dims, ((), ())), preferred_element_type=F32)


def kernel(
    G, C, T,
    act_hbm, q_hbm, do_hbm, wk_hbm, wv_hbm, ses_hbm,
    att_ref, dq_ref, kwg_ref, vwg_ref, ig_ref,
    wall, w2, act, q_in, do_in, ses, arecv, qs, dos, kv, scores, dkv, grecv,
    kvg, kvg_tp, cos_ref, sin_ref, proj, dq_acc,
    loc, w_s, w_r, sb_s, sb_r, z_s, z_r, zf_s, zf_r, a_s, a_r, k_s, k_r,
    d_s, d_r, p_s, p_r, t_s, t_r,
):
    g = lax.axis_index("group")
    c = lax.axis_index("ctx")
    t = lax.axis_index("tp")
    R = act_hbm.shape[0]
    D = act_hbm.shape[1]
    WR = wk_hbm.shape[0]
    CR = min(WR, 512)
    NCH = WR // CR
    DB = D // (G * C)
    DT = D // T
    NK = DT // CR
    H = q_hbm.shape[1] // HD
    scale = 1.0 / math.sqrt(HD)
    is_long = g == 0
    lanes = pl.ds(pl.multiple_of(g * HD, HD), HD)
    olanes = pl.ds(pl.multiple_of((1 - g) * HD, HD), HD)

    def remote(src, dst, ss, rs, **dev):
        return pltpu.make_async_remote_copy(
            src_ref=src, dst_ref=dst, send_sem=ss, recv_sem=rs, device_id=dev, device_id_type=MESH
        )

    def loop(n, f, first=0):
        def step(i, carry):
            f(i)
            return carry

        lax.fori_loop(first, n, step, 0)

    own_rows = pl.ds(pl.multiple_of(c * WR, WR), WR)
    locals_ = [
        pltpu.make_async_copy(wk_hbm, wall.at[own_rows, pl.ds(0, HD)], loc.at[0]),
        pltpu.make_async_copy(wv_hbm, wall.at[own_rows, pl.ds(HD, HD)], loc.at[1]),
        pltpu.make_async_copy(act_hbm, act, loc.at[2]),
        pltpu.make_async_copy(q_hbm, q_in, loc.at[3]),
        pltpu.make_async_copy(do_hbm, do_in, loc.at[4]),
        pltpu.make_async_copy(ses_hbm, ses, loc.at[5]),
    ]
    for one in locals_:
        one.start()

    barrier = pltpu.get_barrier_semaphore()
    me = g * C + c

    def greet_plane(i):
        b = lax.rem(me + i, G * C)
        pl.semaphore_signal(
            barrier, inc=1, device_id={"group": b // C, "ctx": lax.rem(b, C)}, device_id_type=MESH
        )

    def greet_tp(i):
        pl.semaphore_signal(
            barrier, inc=1, device_id={"tp": lax.rem(t + i, T)}, device_id_type=MESH
        )

    loop(G * C, greet_plane, 1)
    loop(T, greet_tp, 1)
    pl.semaphore_wait(barrier, G * C - 1 + T - 1)
    locals_[0].wait()
    locals_[1].wait()

    def rows_of(owner, ch):
        return pl.ds(pl.multiple_of(owner * WR + ch * CR, CR), CR)

    def w_copy(owner, ch, d):
        place = wall.at[rows_of(owner, ch), lanes]
        return remote(
            place, place, w_s.at[d, ch], w_r.at[owner, ch], ctx=lax.rem(c + d, C)
        )

    def send_w(i):
        w_copy(c, i // (C - 1), lax.rem(i, C - 1) + 1).start()

    square = C == 4
    beside = c + 1 - 2 * lax.rem(c, 2)
    across = lax.rem(c + 2, C)
    corner = C - 1 - c

    def near_copy(owner, ch, d, to):
        place = wall.at[rows_of(owner, ch), lanes]
        return remote(place, place, w_s.at[d, ch], w_r.at[owner, ch], ctx=to)

    def relay_copy(ch):
        if ch % 2:
            return near_copy(beside, ch, 3, across)
        return near_copy(across, ch, 3, beside)

    if square:
        for ch in range(NCH):
            near_copy(c, ch, 1, beside).start()
            near_copy(c, ch, 2, across).start()
    else:
        loop(NCH * (C - 1), send_w)

    def sib_copy(owner, ch, which):
        place = wall.at[rows_of(owner, ch), which]
        return remote(place, place, sb_s.at[owner, ch], sb_r.at[owner, ch], group=1 - g)

    def z_target(owner, ch):
        first = owner * WR + ch * CR
        return first // DT, lax.rem(first, DT) // CR

    def z_start(owner, ch):
        to, piece = z_target(owner, ch)

        @pl.when(to != t)
        def _():
            z_copy(owner, ch, to, t, piece).start()

    def z_copy(owner, ch, to, head, piece):
        return remote(
            wall.at[rows_of(owner, ch), lanes],
            w2.at[head, pl.ds(pl.multiple_of(piece * CR, CR), CR), lanes],
            z_s.at[owner, ch], z_r.at[head, piece], tp=to,
        )

    def own_z(ch):
        z_start(c, ch)

    loop(NCH, own_z)

    lane = lax.broadcasted_iota(jnp.int32, (R, HD), 1)
    row = lax.broadcasted_iota(jnp.int32, (R, HD), 0)
    half = lax.rem(lane, HD // 2).astype(F32)
    freq = jnp.exp(half * (-2.0 * math.log(THETA) / HD))
    angle = (row + jnp.where(is_long, c * R, 0)).astype(F32) * freq
    cos_ref[...] = jnp.cos(angle)
    sin_ref[...] = jnp.where(lane < HD // 2, -1.0, 1.0) * jnp.sin(angle)

    def rope(u, sign):
        return u * cos_ref[...] + pltpu.roll(u, HD // 2, 1) * (sin_ref[...] * sign)

    for one in locals_[2:]:
        one.wait()
    for h in range(H):
        cols = slice(h * HD, (h + 1) * HD)
        qs[h] = rope(q_in[:, cols].astype(F32), 1.0).astype(BF)
        dos[h] = do_in[:, cols]

    proj[...] = jnp.zeros_like(proj)

    def project(owner, ch):
        first = pl.multiple_of(owner * WR + ch * CR, CR)
        proj[...] += dot(act[:, pl.ds(first, CR)], wall[rows_of(owner, ch), :], ((1,), (0,)))

    def own_project(ch):
        project(c, ch)

    loop(NCH, own_project)

    def arrived(i):
        ch = i // (C - 1)
        owner = lax.rem(c + C - (lax.rem(i, C - 1) + 1), C)
        w_copy(owner, ch, 1).wait_recv()
        sib_copy(owner, ch, lanes).start()
        z_start(owner, ch)

    def use(i):
        ch = i // (C - 1)
        owner = lax.rem(c + C - (lax.rem(i, C - 1) + 1), C)
        sib_copy(owner, ch, olanes).wait_recv()
        project(owner, ch)

    order = []
    for ch in range(NCH + 1):
        near = [(beside, ch, ch % 2 == 1), (across, ch, ch % 2 == 0)] if ch < NCH else []
        far = [(corner, ch - 1, False)] if ch > 0 else []
        order.append(near + far)

    def chunk(ch):
        loop((ch + 1) * (C - 1), arrived, ch * (C - 1))

        @pl.when(ch > 0)
        def _():
            loop(ch * (C - 1), use, (ch - 1) * (C - 1))

    def take(owner, ch):
        sib_copy(owner, ch, olanes).wait_recv()
        project(owner, ch)

    if square:
        for k, now in enumerate(order):
            for owner, ch, relay in now:
                w_copy(owner, ch, 1).wait_recv()
                if relay:
                    relay_copy(ch).start()
                sib_copy(owner, ch, lanes).start()
                z_start(owner, ch)
            if k > 0:
                for owner, ch, relay in order[k - 1]:
                    take(owner, ch)
    else:
        loop(NCH, chunk)

    def a_copy(i, slot):
        b = lax.rem(me + i, G * C)
        return remote(
            act.at[:, pl.ds(pl.multiple_of(b * DB, DB), DB)],
            arecv.at[pl.ds(pl.multiple_of(slot * R, R), R), :],
            a_s.at[i], a_r.at[slot],
            group=b // C, ctx=lax.rem(b, C),
        )

    def a_start(i):
        a_copy(i, me).start()

    own_a = pltpu.make_async_copy(
        act.at[:, pl.ds(pl.multiple_of(me * DB, DB), DB)],
        arecv.at[pl.ds(pl.multiple_of(me * R, R), R), :],
        loc.at[0],
    )
    own_a.start()
    if square:
        for owner, ch, relay in order[NCH]:
            take(owner, ch)
    else:
        loop(NCH * (C - 1), use, (NCH - 1) * (C - 1))

    kv[c, :, :HD] = rope(proj[:, :HD], 1.0).astype(BF)
    kv[c, :, HD:] = proj[:, HD:].astype(BF)

    def kv_copy(owner, to):
        return remote(kv.at[owner], kv.at[owner], k_s.at[to], k_r.at[owner], ctx=to)

    @pl.when(is_long)
    def _():
        loop(C, lambda to: kv_copy(c, to).start(), c + 1)

    first_block = jnp.where(is_long, 0, c)
    srow = jnp.broadcast_to(ses[...].astype(F32), (R, R))
    same = (srow == srow.T) | is_long
    q_pos = lax.broadcasted_iota(jnp.int32, (R, R), 0)
    k_pos = lax.broadcasted_iota(jnp.int32, (R, R), 1)
    queries = qs[...].reshape(H * R, HD)

    def score_pass(i, top):
        j = c - i + first_block * 0

        @pl.when(j != c)
        def _():
            kv_copy(j, 0).wait_recv()

        s = dot(queries, kv[j, :, :HD], ((1,), (1,))) * scale
        allowed = same & (k_pos <= q_pos + (c - j) * R)
        s = jnp.where(allowed[None], s.reshape(H, R, R), -jnp.inf).reshape(H * R, R)
        scores[j] = s
        return jnp.maximum(top, jnp.max(s, 1, keepdims=True))

    count = c + 1 - first_block
    top = lax.fori_loop(0, count, score_pass, jnp.full((H * R, 1), -jnp.inf, F32))
    loop(G * C // 2, a_start, 1)

    def sum_pass(j, total):
        return total + jnp.sum(jnp.exp(scores[j] - top), 1, keepdims=True)

    total = lax.fori_loop(first_block, c + 1, sum_pass, jnp.zeros((H * R, 1), F32))
    log_total = top + jnp.log(total)

    dq_acc[...] = jnp.zeros_like(dq_acc)

    def out_pass(j):
        w = jnp.exp(scores[j] - log_total)
        scores[j] = w
        dq_acc[...] += dot(w.astype(BF), kv[j, :, HD:], ((1,), (0,)))

    loop(c + 1, out_pass, first_block)
    attended = dq_acc[...].astype(BF)
    for h in range(H):
        att_ref[:, h * HD:(h + 1) * HD] = attended[h * R:(h + 1) * R]
    grads = dos[...].reshape(H * R, HD)
    out_dot = jnp.sum(grads.astype(F32) * attended.astype(F32), 1, keepdims=True)
    dq_acc[...] = jnp.zeros_like(dq_acc)

    def d_copy(owner, source):
        return remote(dkv.at[owner], grecv.at[source], d_s.at[owner], d_r.at[source], ctx=owner)

    def grad_pass(j):
        w = scores[j]
        prob_grad = dot(grads, kv[j, :, HD:], ((1,), (1,)))
        ds = (w * (prob_grad - out_dot)).astype(BF)
        dkv[j, :, :HD] = dot(ds, queries, ((0,), (0,))) * scale
        dkv[j, :, HD:] = dot(w.astype(BF), grads, ((0,), (0,)))

        @pl.when(j != c)
        def _():
            d_copy(j, c).start()

        dq_acc[...] += dot(ds, kv[j, :, :HD], ((1,), (0,)))

    loop(c + 1, grad_pass, first_block)
    loop(G * C, a_start, G * C // 2)
    for h in range(H):
        turned = rope(dq_acc[h * R:(h + 1) * R] * scale, -1.0)
        dq_ref[:, h * HD:(h + 1) * HD] = turned.astype(BF)

    proj[...] = dkv[c]

    def add_grad(source):
        d_copy(0, source).wait_recv()
        proj[...] += grecv[source]

    @pl.when(is_long)
    def _():
        loop(C, add_grad, c + 1)

    my_rows = pl.ds(pl.multiple_of(me * R, R), R)
    kvg[my_rows, :HD] = rope(proj[:, :HD], -1.0).astype(BF)
    kvg[my_rows, HD:] = proj[:, HD:].astype(BF)

    def p_copy(i, slot):
        b = lax.rem(me + i, G * C)
        rows = pl.ds(pl.multiple_of(slot * R, R), R)
        return remote(
            kvg.at[rows], kvg.at[rows], p_s.at[i], p_r.at[slot], group=b // C, ctx=lax.rem(b, C)
        )

    def t_copy(i, slot):
        return remote(kvg.at[my_rows], kvg_tp.at[slot], t_s.at[i], t_r.at[slot], tp=lax.rem(t + i, T))

    loop(T, lambda i: t_copy(i, t).start(), 1)
    loop(G * C, lambda i: p_copy(i, me).start(), 1)

    def zf_copy(head, piece, which):
        place = w2.at[head, pl.ds(pl.multiple_of(piece * CR, CR), CR), which]
        return remote(place, place, zf_s.at[head, piece], zf_r.at[head, piece], group=1 - g)

    def z_arrived(i):
        head = lax.rem(t + 1 + i // NK, T)
        piece = lax.rem(i, NK)
        z_copy(0, 0, 0, head, piece).wait_recv()
        zf_copy(head, piece, lanes).start()

    loop((T - 1) * NK, z_arrived)

    loop(T, lambda i: t_copy(0, lax.rem(t + i, T)).wait_recv(), 1)

    def z_wait(i):
        zf_copy(lax.rem(t + 1 + i // NK, T), lax.rem(i, NK), olanes).wait_recv()

    loop((T - 1) * NK, z_wait)

    def igrad(i):
        at = pl.multiple_of(i * CR, CR)
        own = wall[pl.ds(pl.multiple_of(t * DT + i * CR, CR), CR), :]
        result = dot(kvg[my_rows, :], own, ((1,), (1,)))
        for d in range(1, T):
            head = lax.rem(t + d, T)
            result += dot(kvg_tp[head], w2[head, pl.ds(at, CR), :], ((1,), (1,)))
        ig_ref[:, pl.ds(at, CR)] = result.astype(BF)

    loop(NK, igrad)

    own_a.wait()

    def a_wait(i):
        slot = lax.rem(me + i, G * C)
        a_copy(0, slot).wait_recv()
        p_copy(0, slot).wait_recv()

    loop(G * C, a_wait, 1)
    step = min(DB, 256)

    def wgrad(i):
        at = pl.ds(pl.multiple_of(i * step, step), step)
        both = dot(arecv[:, at], kvg[...], ((0,), (0,)))
        kwg_ref[at, :] = both[:, :HD]
        vwg_ref[at, :] = both[:, HD:]

    loop(DB // step, wgrad)

    if square:
        for ch in range(NCH):
            near_copy(c, ch, 1, beside).wait_send()
            near_copy(c, ch, 2, across).wait_send()
            relay_copy(ch).wait_send()
    else:
        loop(NCH * (C - 1), lambda i: w_copy(c, i // (C - 1), lax.rem(i, C - 1) + 1).wait_send())

    def sent_chunk(i):
        owner = i // NCH
        ch = lax.rem(i, NCH)

        @pl.when(owner != c)
        def _():
            sib_copy(owner, ch, lanes).wait_send()

        to, piece = z_target(owner, ch)

        @pl.when(to != t)
        def _():
            z_copy(owner, ch, to, t, piece).wait_send()

    loop(C * NCH, sent_chunk)
    loop(G * C, lambda i: a_copy(i, me).wait_send(), 1)
    loop(G * C, lambda i: p_copy(i, me).wait_send(), 1)
    loop(T, lambda i: t_copy(i, t).wait_send(), 1)
    loop((T - 1) * NK, lambda i: zf_copy(
        lax.rem(t + 1 + i // NK, T), lax.rem(i, NK), lanes).wait_send())

    @pl.when(is_long)
    def _():
        loop(C, lambda to: kv_copy(c, to).wait_send(), c + 1)
        loop(c, lambda owner: d_copy(owner, c).wait_send())


def copy_kernel(n, *refs):
    sems = refs[2 * n]
    hold = refs[2 * n + 1:]
    come = [pltpu.make_async_copy(refs[k], hold[k], sems.at[k]) for k in range(n)]
    leave = [pltpu.make_async_copy(hold[k], refs[n + k], sems.at[n + k]) for k in range(n)]
    for one in come:
        one.start()
    for k in range(n):
        come[k].wait()
        leave[k].start()
    for one in leave:
        one.wait()


def hand_out(arrays):
    n = len(arrays)
    any_ = pl.BlockSpec(memory_space=pl.ANY)
    return pl.pallas_call(
        functools.partial(copy_kernel, n),
        out_shape=tuple(jax.ShapeDtypeStruct(a.shape, a.dtype) for a in arrays),
        in_specs=[any_] * n,
        out_specs=(any_,) * n,
        scratch_shapes=[pltpu.SemaphoreType.DMA((2 * n,))] + [pltpu.VMEM(a.shape, a.dtype) for a in arrays],
    )(*arrays)


def body(sizes, activations, queries, out_grad, key_weight, value_weight, sessions):
    G, C, T = sizes
    R, D = activations.shape
    WR = key_weight.shape[0]
    QC = queries.shape[1]
    H = QC // HD
    CR = min(WR, 512)
    NCH = WR // CR
    DB = D // (G * C)
    DT = D // T
    NK = DT // CR
    any_ = pl.BlockSpec(memory_space=pl.ANY)
    vmem = pl.BlockSpec(memory_space=pltpu.VMEM)
    dma = pltpu.SemaphoreType.DMA
    V = pltpu.VMEM
    made = pl.pallas_call(
        functools.partial(kernel, G, C, T),
        out_shape=(
            jax.ShapeDtypeStruct((R, QC), BF),
            jax.ShapeDtypeStruct((R, QC), BF),
            jax.ShapeDtypeStruct((DB, HD), F32),
            jax.ShapeDtypeStruct((DB, HD), F32),
            jax.ShapeDtypeStruct((R, DT), BF),
        ),
        in_specs=[any_] * 6,
        out_specs=(vmem,) * 5,
        scratch_shapes=[
            V((D, 2 * HD), BF), V((T, DT, 2 * HD), BF), V((R, D), BF), V((R, QC), BF),
            V((R, QC), BF), V((1, R), jnp.int32), V((G * C * R, DB), BF), V((H, R, HD), BF),
            V((H, R, HD), BF), V((C, R, 2 * HD), BF), V((C, H * R, R), F32),
            V((C, R, 2 * HD), F32), V((C, R, 2 * HD), F32),
            V((G * C * R, 2 * HD), BF), V((T, R, 2 * HD), BF),
            V((R, HD), F32), V((R, HD), F32), V((R, 2 * HD), F32), V((H * R, HD), F32),
            dma((6,)),
            dma((C, NCH)), dma((C, NCH)), dma((C, NCH)), dma((C, NCH)),
            dma((C, NCH)), dma((T, NK)), dma((T, NK)), dma((T, NK)),
            dma((G * C,)), dma((G * C,)), dma((C,)), dma((C,)),
            dma((C,)), dma((C,)), dma((G * C,)), dma((G * C,)), dma((T,)), dma((T,)),
        ],
        compiler_params=pltpu.CompilerParams(
            collective_id=0, has_side_effects=True, vmem_limit_bytes=58 * 1024 * 1024
        ),
    )(activations, queries, out_grad, key_weight, value_weight, sessions)
    return hand_out(made)


def solution(mesh):
    rows = ("group", "ctx")
    sizes = tuple(mesh.shape[name] for name in ("group", "ctx", "tp"))
    return jax.shard_map(
        functools.partial(body, sizes),
        mesh=mesh,
        in_specs=(
            P(rows, None), P(rows, "tp"), P(rows, "tp"),
            P("ctx", "tp"), P("ctx", "tp"), P("ctx", None),
        ),
        out_specs=(P(rows, "tp"),) * 5,
        check_vma=False,
    )
```
